256 devices in a mesh: lon: 64 (over x, z, y_lo), lat: 4 (over y_hi, core).
Axes of the slice: x: 4, y: 4 (y_hi: 2, y_lo: 2; y = y_hi * 2 + y_lo), z: 8, core: 2. Of those that a mesh axis runs over, the one named last changes fastest.
Arguments:
- wind: float32 [2, 24, 64, 8192], P(None, None, 'lat', 'lon'), may hold values from -3 to 6
- tracers: float32 [4, 24, 64, 8192], P(None, None, 'lat', 'lon'), may hold values from -6 to 6
- cell_off: int32 [2, 24, 64, 8192], P(None, None, 'lat', 'lon'), may hold values from -2 to 6, as said below
Outputs:
- advected: float32 [6, 24, 64, 8192], P(None, None, 'lat', 'lon')
The draws below stay inside these ranges and needn't reach their ends.
Inputs may be any that keep to these rules, and one draw needn't show every extreme that they name: `cell_off`: column offsets lie in -2 to 6 and row offsets in -2 to 2; both ends of each are taken in every draw.
All inputs are finite; a program needn't handle non-finite values.
Results may differ from the reference program's by a relative error of at most 0.0003.
Values sent between devices are 32-bit elements; how exact they have to be, the bound alone decides.
No kernel may reach another device: no remote copies, remote signals or barrier semaphores. Data moves between devices by JAX's collectives and lax.ppermute only.
A program may use at most 128 MiB of HBM per device.

```python
import jax
import jax.numpy as jnp
from jax import lax

LEV = 24
MAXOFF = 6
NLAT = 64
NLON = 8192


def offsets_from(key):
    first, second = jax.random.split(key)
    col_off = jax.random.randint(first, (LEV, NLAT, NLON), -2, MAXOFF + 1)
    row_off = jax.random.randint(second, (LEV, NLAT, NLON), -2, 3)
    col_off = col_off.at[:, 0, 0].set(MAXOFF).at[:, 0, 1].set(-2)
    row_off = row_off.at[:, 0, 0].set(2).at[:, 0, 1].set(-2)
    return jnp.stack([col_off, row_off]).astype(jnp.int32)


def draw_cell_off(key, part):
    return offsets_from(key)


def draw_wind(key, part):
    offsets = offsets_from(key).astype(jnp.float32)
    key = jax.random.fold_in(key, 7)
    frac = jax.random.uniform(key, offsets.shape, jnp.float32, 0.05, 0.95)
    return offsets - frac


def block_scale(rng, dims, shards, least, largest):
    level = 1.0
    for position, parts in shards:
        draws = jax.random.uniform(jax.random.fold_in(jax.random.fold_in(rng, 6), position), (parts,), jnp.float32, least / len(shards), largest / len(shards))
        level = level * jnp.repeat(jnp.exp(draws), dims[position] // parts).reshape((-1,) + (1,) * (len(dims) - 1 - position))
    return level


def bell_draw(stream_key, extent, deviation, limit, shards=(), kind=jnp.bfloat16):
    loudness = block_scale(stream_key, extent, shards, -0.22, 0.18) if shards else 1.0
    entries = jax.random.normal(stream_key, extent, jnp.float32) * deviation * loudness
    return jnp.minimum(jnp.maximum(entries, -limit), limit).astype(kind)


def setup_inputs(seed: int = 0) -> dict:
    seeds = jax.random.split(jax.random.key(seed), 4)
    wind = draw_wind(jax.random.fold_in(seeds[3], 71), 0)
    tracers = bell_draw(seeds[1], (4, LEV, NLAT, NLON), 1.0, 6.0, ((2, 4), (3, 64)), jnp.float32)
    cell_off = draw_cell_off(jax.random.fold_in(seeds[3], 71), 0)
    return dict(wind=wind, tracers=tracers, cell_off=cell_off)


def sample(padded, row_index, col_index):
    chans, levels, height, breadth = padded.shape
    flat = padded.reshape(chans, levels, height * breadth)
    index = (row_index * breadth + col_index).reshape(1, levels, -1)
    index = jnp.broadcast_to(index, (chans, levels, index.shape[-1]))
    picked = jnp.take_along_axis(flat, index, axis=2)
    return picked.reshape((chans,) + row_index.shape)


def cubic_weights(frac):
    return (-frac * (frac - 1.0) * (frac - 2.0) / 6.0,
            (frac + 1.0) * (frac - 1.0) * (frac - 2.0) / 2.0,
            -(frac + 1.0) * frac * (frac - 2.0) / 2.0,
            (frac + 1.0) * frac * (frac - 1.0) / 6.0)


def advect(wind_pad, tracer_pad, wind, col_off, row_off, row_base, col_base):
    col_float = col_off.astype(jnp.float32)
    row_float = row_off.astype(jnp.float32)
    disp_east = wind[0]
    disp_north = wind[1]
    for repeat in range(2):
        frac_x = jnp.clip(col_float - disp_east, 0.0, 1.0)
        frac_y = jnp.clip(row_float - disp_north, 0.0, 1.0)
        low_left = sample(wind_pad, row_base, col_base)
        low_right = sample(wind_pad, row_base, col_base + 1)
        up_left = sample(wind_pad, row_base + 1, col_base)
        up_right = sample(wind_pad, row_base + 1, col_base + 1)
        depart = (1.0 - frac_y) * ((1.0 - frac_x) * low_left + frac_x * low_right) + frac_y * ((1.0 - frac_x) * up_left + frac_x * up_right)
        disp_east = 0.5 * (wind[0] + depart[0])
        disp_north = 0.5 * (wind[1] + depart[1])
    frac_x = jnp.clip(col_float - disp_east, 0.0, 1.0)
    frac_y = jnp.clip(row_float - disp_north, 0.0, 1.0)
    weight_x = cubic_weights(frac_x)
    weight_y = cubic_weights(frac_y)
    results = []
    for padded in (wind_pad, tracer_pad):
        total = None
        for row_step in range(4):
            inner = None
            for col_step in range(4):
                term = weight_x[col_step] * sample(padded, row_base + row_step - 1, col_base + col_step - 1)
                inner = term if inner is None else inner + term
            outer = weight_y[row_step] * inner
            total = outer if total is None else total + outer
        results.append(total)
    return jnp.concatenate(results, axis=0)


def pad_global(fields):
    west = MAXOFF + 1
    wide = jnp.concatenate([fields[..., NLON - west:], fields, fields[..., :4]], axis=-1)
    return jnp.pad(wide, ((0, 0), (0, 0), (4, 4), (0, 0)))


def reference(wind, tracers, cell_off):
    west = MAXOFF + 1
    rows = jnp.arange(NLAT, dtype=jnp.int32)[:, None]
    cols = jnp.arange(NLON, dtype=jnp.int32)[None, :]

    def one_level(level):
        wind_lev = lax.dynamic_slice_in_dim(wind, level, 1, 1)
        tracer_lev = lax.dynamic_slice_in_dim(tracers, level, 1, 1)
        off_lev = lax.dynamic_slice_in_dim(cell_off, level, 1, 1)
        row_base = (rows - off_lev[1] + 4).astype(jnp.int32)
        col_base = (cols - off_lev[0] + west).astype(jnp.int32)
        return advect(pad_global(wind_lev), pad_global(tracer_lev), wind_lev, off_lev[0], off_lev[1], row_base, col_base)[:, 0]

    stacked = lax.map(one_level, jnp.arange(LEV, dtype=jnp.int32))
    return jnp.transpose(stacked, (1, 0, 2, 3))
```

```python
import functools

import jax
import jax.numpy as jnp
from jax import lax
from jax.experimental import pallas as pl
from jax.experimental.pallas import tpu as pltpu
from jax.sharding import PartitionSpec as P

LEVS = 24
ROWS = 16
COLS = 128
FIELDS = 6
GROUPS = 3
PAIRS = FIELDS * LEVS // 2
EDGE = FIELDS * GROUPS
T_EDGE = 8 * (PAIRS + 2)
T_ROWS = T_EDGE + 8 * (2 * EDGE // 4)
PAD_ROWS = 32
VMEM_LIMIT = 48 * 1024 * 1024


def parities():
    return lax.axis_index("lon") % 2 == 0, lax.axis_index("lat") % 2 == 0


def pick(flag, first, second):
    return jnp.where(jnp.full(first.shape, flag), first, second)


def lane_slot(shape):
    return lax.broadcasted_iota(jnp.int32, shape, len(shape) - 1) % 16


def pack_kernel(wind_ref, tracer_ref, sa_ref, sb_ref, t1_ref, t2_ref):
    lon_even, lat_even = parities()
    low_half = lax.broadcasted_iota(jnp.int32, (8, COLS), 0) < 4
    zero = jnp.zeros((8, COLS), jnp.float32)
    for t_ref in (t1_ref, t2_ref):
        t_ref[0:8] = zero
        t_ref[8 * (PAIRS + 1) : T_EDGE] = zero

    def field_rows(ref, base, count):
        def step(pair, carry):
            field = pair // (LEVS // 2)
            lev = 2 * (pair % (LEVS // 2))
            first = ref[field, lev]
            second = ref[field, lev + 1]
            top = jnp.where(low_half, first[0:8], pltpu.roll(second[0:8], 4, 0))
            bottom = jnp.where(low_half, pltpu.roll(first[8:16], 4, 0), second[8:16])
            start = pl.multiple_of(8 * (base + pair + 1), 8)
            t1_ref[pl.ds(start, 8)] = pick(lat_even, bottom, top)
            t2_ref[pl.ds(start, 8)] = pick(lat_even, top, bottom)
            return carry

        lax.fori_loop(0, count, step, 0, unroll=4)

    field_rows(wind_ref, 0, LEVS)
    field_rows(tracer_ref, LEVS, 2 * LEVS)
    for field in range(FIELDS):
        ref, inner = (wind_ref, field) if field < 2 else (tracer_ref, field - 2)
        for group in range(GROUPS):
            turned = ref[inner, 8 * group : 8 * group + 8].reshape(COLS, COLS).T
            west = turned[0:8]
            east = turned[COLS - 8 : COLS]
            sa_ref[GROUPS * field + group] = pick(lon_even, east, west)
            sb_ref[GROUPS * field + group] = pick(lon_even, west, east)


def corner_kernel(sa_ref, sb_ref, t1_in, t2_in, t1_ref, t2_ref, buf1, buf2, sem1, sem2):
    lon_even, lat_even = parities()
    slot = lane_slot((8, COLS))
    halos = []
    for edge in range(EDGE):
        halos.append(pick(lon_even, sb_ref[edge], sa_ref[edge]))
    for edge in range(EDGE):
        halos.append(pick(lon_even, sa_ref[edge], sb_ref[edge]))
    for packed in range(2 * EDGE // 4):
        top = None
        bottom = None
        for part in range(4):
            piece = halos[4 * packed + part]
            upper = pltpu.roll(piece, 4 * part, 1) if part else piece
            lower = pltpu.roll(piece, (4 * part - 12) % COLS, 1) if part != 3 else piece
            here = (slot >= 4 * part) & (slot < 4 * part + 4)
            top = upper if top is None else jnp.where(here, upper, top)
            bottom = lower if bottom is None else jnp.where(here, lower, bottom)
        buf1[8 * packed : 8 * packed + 8] = pick(lat_even, bottom, top)
        buf2[8 * packed : 8 * packed + 8] = pick(lat_even, top, bottom)
    copy1 = pltpu.make_async_copy(buf1, t1_ref.at[pl.ds(T_EDGE, T_ROWS - T_EDGE)], sem1)
    copy2 = pltpu.make_async_copy(buf2, t2_ref.at[pl.ds(T_EDGE, T_ROWS - T_EDGE)], sem2)
    copy1.start()
    copy2.start()
    copy1.wait()
    copy2.wait()


def cubic_weights(frac):
    return (
        -frac * (frac - 1.0) * (frac - 2.0) * (1.0 / 6.0),
        (frac + 1.0) * (frac - 1.0) * (frac - 2.0) * 0.5,
        (frac + 1.0) * frac * (frac - 2.0) * -0.5,
        (frac + 1.0) * frac * (frac - 1.0) * (1.0 / 6.0),
    )


def rotated(weights, odd, half):
    once = [jnp.where(odd, weights[(k - 1) % 4], weights[k]) for k in range(4)]
    return [jnp.where(half, once[(k - 2) % 4], once[k]) for k in range(4)]


def middle_pair(values, odd, half):
    one = jnp.where(half, values[3], values[1])
    two = jnp.where(half, values[0], values[2])
    three = jnp.where(half, values[1], values[3])
    return jnp.where(odd, two, one), jnp.where(odd, three, two)


def advect_block(load, col_off, row_off, wind_here, emit):
    row_start = 2 - row_off
    col_start = 6 - col_off
    row_low = [row_start <= p for p in range(4)]
    col_low = [col_start <= q for q in range(4)]
    col_mid = [col_start <= q + 4 for q in range(4)]
    row_odd = (row_start & 1) != 0
    row_half = (row_start & 2) != 0
    col_odd = (col_start & 1) != 0
    col_half = (col_start & 2) != 0

    def column_class(field, q):
        picked = []
        for p in range(4):
            parts = [
                jnp.where(row_low[p], load(field, p, k), load(field, p + 4, k))
                for k in (q, q + 4, q + 8)
            ]
            picked.append(
                jnp.where(col_low[q], parts[0], jnp.where(col_mid[q], parts[1], parts[2]))
            )
        return picked

    col_float = col_off.astype(jnp.float32)
    row_float = row_off.astype(jnp.float32)
    wind_taps = [[column_class(field, q) for q in range(4)] for field in range(2)]
    cells = []
    for field in range(2):
        lows = []
        highs = []
        for q in range(4):
            low, high = middle_pair(wind_taps[field][q], row_odd, row_half)
            lows.append(low)
            highs.append(high)
        low_left, low_right = middle_pair(lows, col_odd, col_half)
        up_left, up_right = middle_pair(highs, col_odd, col_half)
        cells.append((low_left, low_right - low_left, up_left, up_right - up_left))
    disp = wind_here
    for repeat in range(2):
        frac_x = jnp.clip(col_float - disp[0], 0.0, 1.0)
        frac_y = jnp.clip(row_float - disp[1], 0.0, 1.0)
        moved = []
        for field in range(2):
            low_left, low_step, up_left, up_step = cells[field]
            low = low_left + frac_x * low_step
            up = up_left + frac_x * up_step
            depart = low + frac_y * (up - low)
            moved.append(0.5 * (wind_here[field] + depart))
        disp = moved
    frac_x = jnp.clip(col_float - disp[0], 0.0, 1.0)
    frac_y = jnp.clip(row_float - disp[1], 0.0, 1.0)
    col_weights = rotated(cubic_weights(frac_x), col_odd, col_half)
    row_weights = rotated(cubic_weights(frac_y), row_odd, row_half)
    for field in range(FIELDS):
        sums = [None] * 4
        for q in range(4):
            taps = wind_taps[field][q] if field < 2 else column_class(field, q)
            for p in range(4):
                term = col_weights[q] * taps[p]
                sums[p] = term if sums[p] is None else sums[p] + term
        total = row_weights[0] * sums[0]
        for p in range(1, 4):
            total = total + row_weights[p] * sums[p]
        emit(field, total)


def main_kernel(
    wind_ref, tracer_ref, off_ref, sa_ref, sb_ref, t1_ref, t2_ref, out_ref, rows, halo, shifted, turned_off, turned_out
):
    lon_even, lat_even = parities()
    slot = lane_slot((8, COLS))

    def fill(ref, base, count):
        def step(index, carry):
            lev = index % LEVS
            whole = base + index
            own = ref[index // LEVS, lev]
            start = pl.multiple_of(whole * PAD_ROWS, PAD_ROWS)
            rows[pl.ds(start + 8, 16)] = own
            first = t1_ref[pl.ds(4 * whole + 4, 8)]
            second = t2_ref[pl.ds(4 * whole + 4, 8)]
            rows[pl.ds(start, 8)] = pick(lat_even, second, first)
            first = t1_ref[pl.ds(4 * whole + 8, 8)]
            second = t2_ref[pl.ds(4 * whole + 8, 8)]
            rows[pl.ds(start + 24, 8)] = pick(lat_even, first, second)
            return carry

        lax.fori_loop(0, count, step, 0, unroll=4)

    fill(wind_ref, 0, 2 * LEVS)
    fill(tracer_ref, 2 * LEVS, 4 * LEVS)
    for packed in range(2 * EDGE // 4):
        start = T_EDGE + 8 * packed
        first = t1_ref[start : start + 8]
        second = t2_ref[start : start + 8]
        north = pick(lat_even, second, first)
        south = pick(lat_even, first, second)
        for part in range(4):
            above = pltpu.roll(north, (-4 - 4 * part) % COLS, 1)
            below = pltpu.roll(south, 16 - 4 * part, 1)
            halo[4 * packed + part] = jnp.where(slot >= 12, above, below)

    def build(group, place, unit):
        field = unit // 8
        row = unit % 8
        base = (field * LEVS + 8 * group) * PAD_ROWS + row + 5
        block = jnp.concatenate([rows[pl.ds(base + lev * PAD_ROWS, 16)] for lev in range(8)], axis=0)
        shifted[place, field, row, 8 : 8 + COLS] = block.T
        edge = GROUPS * field + group
        outside = (slot < row - 3) | (slot > row + 12)
        from_a = sa_ref[edge]
        from_b = sb_ref[edge]
        west = jnp.where(outside, halo[edge], pick(lon_even, from_b, from_a))
        east = jnp.where(outside, halo[EDGE + edge], pick(lon_even, from_a, from_b))
        turn = (3 - row) % COLS
        shifted[place, field, row, 0:8] = pltpu.roll(west, turn, 1)
        shifted[place, field, row, 8 + COLS : 16 + COLS] = pltpu.roll(east, turn, 1)

    def build_off(group, place):
        for part in range(2):
            block = off_ref[part, 8 * group : 8 * group + 8].reshape(COLS, COLS)
            turned_off[place, part] = block.T

    def compute(place, block):
        start = pl.multiple_of(8 * block, 8)

        def load(field, row, k):
            return shifted[place, field, row, pl.ds(start + 1 + k, 8)]

        def emit(field, value):
            turned_out[field, pl.ds(start, 8)] = value

        here = [shifted[place, field, 3, pl.ds(start + 8, 8)] for field in range(2)]
        advect_block(
            load, turned_off[place, 0, pl.ds(start, 8)], turned_off[place, 1, pl.ds(start, 8)], here, emit
        )

    build_off(0, 0)

    def first_units(unit, carry):
        build(0, 0, unit)
        return carry

    lax.fori_loop(0, 48, first_units, 0, unroll=2)
    for group in range(GROUPS):
        place = group % 2
        last = group + 1 == GROUPS
        if not last:
            build_off(group + 1, 1 - place)

        def step(block, carry):
            if not last:
                for part in range(3):
                    build(group + 1, 1 - place, 3 * block + part)
            compute(place, block)
            return carry

        lax.fori_loop(0, 16, step, 0)
        for field in range(FIELDS):
            out_ref[field, 8 * group : 8 * group + 8] = turned_out[field].T.reshape(8, ROWS, COLS)


def shards(wind, tracers, cell_off):
    f32 = jnp.float32
    vmem = pl.BlockSpec(memory_space=pltpu.VMEM)
    anywhere = pl.BlockSpec(memory_space=pl.ANY)
    params = pltpu.CompilerParams(vmem_limit_bytes=VMEM_LIMIT)
    edge_shape = jax.ShapeDtypeStruct((EDGE, 8, COLS), f32)
    t_shape = jax.ShapeDtypeStruct((T_ROWS, COLS), f32)
    sa, sb, t1, t2 = pl.pallas_call(
        pack_kernel,
        out_shape=(edge_shape, edge_shape, t_shape, t_shape),
        in_specs=[vmem] * 2,
        out_specs=(vmem,) * 4,
        compiler_params=params,
        name="pack",
    )(wind, tracers)
    count = lax.axis_size("lon")
    lon_first = [(i, i ^ 1) for i in range(count)]
    lon_second = [(i, (i + 1) % count if i % 2 else (i - 1) % count) for i in range(count)]
    lats = lax.axis_size("lat")
    lat_first = [(i, i ^ 1) for i in range(lats)]
    lat_second = [(i, i + 1 if i % 2 else i - 1) for i in range(1, lats - 1)]
    sa = lax.ppermute(sa, "lon", lon_first)
    sb = lax.ppermute(sb, "lon", lon_second)
    t1, t2 = pl.pallas_call(
        corner_kernel,
        out_shape=(t_shape, t_shape),
        in_specs=[vmem, vmem, anywhere, anywhere],
        out_specs=(anywhere, anywhere),
        scratch_shapes=[
            pltpu.VMEM((T_ROWS - T_EDGE, COLS), f32),
            pltpu.VMEM((T_ROWS - T_EDGE, COLS), f32),
            pltpu.SemaphoreType.DMA,
            pltpu.SemaphoreType.DMA,
        ],
        input_output_aliases={2: 0, 3: 1},
        compiler_params=params,
        name="corners",
    )(sa, sb, t1, t2)
    t1 = lax.ppermute(t1, "lat", lat_first)
    t2 = lax.ppermute(t2, "lat", lat_second)
    return pl.pallas_call(
        main_kernel,
        out_shape=jax.ShapeDtypeStruct((FIELDS, LEVS, ROWS, COLS), f32),
        in_specs=[vmem] * 7,
        out_specs=vmem,
        scratch_shapes=[
            pltpu.VMEM((FIELDS * LEVS * PAD_ROWS, COLS), f32),
            pltpu.VMEM((2 * EDGE, 8, COLS), f32),
            pltpu.VMEM((2, FIELDS, 8, COLS + 16, COLS), f32),
            pltpu.VMEM((2, 2, COLS, COLS), jnp.int32),
            pltpu.VMEM((FIELDS, COLS, COLS), f32),
        ],
        compiler_params=params,
        name="advect",
    )(wind, tracers, cell_off, sa, sb, t1, t2)


def solution(mesh):
    placed = P(None, None, "lat", "lon")
    return jax.shard_map(shards, mesh=mesh, in_specs=(placed,) * 3, out_specs=placed, check_vma=False)
```

```python
import jax
import jax.numpy as jnp
from jax import lax
from jax.experimental import pallas as pl
from jax.experimental.pallas import tpu as pltpu
from jax.sharding import PartitionSpec as P

LEVS = 24
ROWS = 16
COLS = 128
WINDS = 2
FIELDS = 6
GROUPS = 3
EDGE = FIELDS * GROUPS
WIDE = COLS + 16
DEPTH = 3 * COLS
SIDE = -(-EDGE // 4)
MAIN = 8 * (FIELDS * LEVS // 2 + 2)
NARROW = 2 * 8 * SIDE
PAYLOAD = EDGE + 2 * SIDE
STRIP = 24
TALL = COLS + 8
EARLY = 16
VMEM_LIMIT = 24 * 1024 * 1024
PACK_LIMIT = 60 * 1024 * 1024


def parities():
    return lax.axis_index("lon") % 2 == 0, lax.axis_index("lat") % 2 == 0


def pick(flag, first, second):
    return jnp.where(jnp.full(first.shape, flag), first, second)


def lane_slot(shape):
    return lax.broadcasted_iota(jnp.int32, shape, len(shape) - 1) % 16


def split(values):
    high = values.astype(jnp.bfloat16)
    return high, (values - high.astype(jnp.float32)).astype(jnp.bfloat16)


def whole(values):
    return values.astype(jnp.bfloat16).astype(jnp.float32)


def load_fields(wind_hbm, tracer_hbm, cells, sems):
    copies = []
    for field in range(FIELDS):
        source = wind_hbm.at[field] if field < WINDS else tracer_hbm.at[field - WINDS]
        copies.append(pltpu.make_async_copy(source, cells.at[field], sems.at[field]))
    for copy in copies:
        copy.start()
    return copies


def pack_kernel(wind_hbm, tracer_hbm, edges, t1_ref, t2_ref, cells, sems):
    lat_even = parities()[1]
    low_half = lax.broadcasted_iota(jnp.int32, (8, COLS), 0) < 4
    slot = lane_slot((8, COLS))
    zero = jnp.zeros((8, COLS), jnp.float32)
    copies = load_fields(wind_hbm, tracer_hbm, cells, sems)

    def put(start, top, bottom):
        t1_ref[start : start + 8] = pick(lat_even, bottom, top)
        t2_ref[start : start + 8] = pick(lat_even, top, bottom)

    put(0, zero, zero)
    put(MAIN - 8, zero, zero)
    for field in range(FIELDS):
        copies[field].wait()
        for group in range(GROUPS):
            turned = cells[field, 8 * group : 8 * group + 8].reshape(COLS, COLS).T
            edges[GROUPS * field + group] = turned[0:8]
            edges[EDGE + GROUPS * field + group] = turned[COLS - 8 : COLS]
        for pair in range(LEVS // 2):
            first = cells[field, 2 * pair]
            second = cells[field, 2 * pair + 1]
            top = jnp.where(low_half, first[0:8], pltpu.roll(second[0:8], 4, 0))
            bottom = jnp.where(low_half, pltpu.roll(first[8:16], 4, 0), second[8:16])
            put(8 * (field * LEVS // 2 + pair + 1), top, bottom)
    for side in range(2):
        for packed in range(SIDE):
            top = None
            bottom = None
            for part in range(min(4, EDGE - 4 * packed)):
                piece = edges[EDGE * side + 4 * packed + part]
                upper = pltpu.roll(piece, 4 * part, 1) if part else piece
                lower = pltpu.roll(piece, (4 * part - 12) % COLS, 1) if part != 3 else piece
                here = (slot >= 4 * part) & (slot < 4 * part + 4)
                top = upper if top is None else jnp.where(here, upper, top)
                bottom = lower if bottom is None else jnp.where(here, lower, bottom)
            put(MAIN + 8 * (SIDE * side + packed), top, bottom)


def side_kernel(edges, t1_ref, t2_ref, a_ref, forth_ref, back_ref):
    lon_even, lat_even = parities()

    def put(place, west, east):
        a_ref[place] = pick(lon_even, east, west)
        other = pick(lon_even, west, east)
        forth_ref[place] = other
        back_ref[place] = other

    for edge in range(EDGE):
        put(edge, edges[edge], edges[EDGE + edge])
    for packed in range(SIDE):
        north = []
        south = []
        for side in range(2):
            start = MAIN + 8 * (SIDE * side + packed)
            first = t1_ref[start : start + 8]
            second = t2_ref[start : start + 8]
            north.append(pick(lat_even, second, first))
            south.append(pick(lat_even, first, second))
        put(EDGE + packed, *north)
        put(EDGE + SIDE + packed, *south)


def own_kernel(wind_ref, tracer_ref, off_ref, own_ref, turned_off, matrix_ref):
    for field in range(FIELDS):
        ref, inner = (wind_ref, field) if field < WINDS else (tracer_ref, field - WINDS)
        for group in range(GROUPS):
            turned = ref[inner, 8 * group : 8 * group + 8].reshape(COLS, COLS).T
            own_ref[GROUPS * field + group] = jnp.concatenate(split(turned), axis=1)
    source = lax.broadcasted_iota(jnp.int32, (COLS, COLS), 0)
    target = lax.broadcasted_iota(jnp.int32, (COLS, COLS), 1)
    source_slot = source % 16
    beside = jnp.where(source_slot < 8, 16 + source_slot % 4, source_slot % 4 - 4)
    same = source // 16 == target // 16
    for shift in range(8):
        wanted = target % 16 + (shift - 3)
        inside = jnp.where(same & (source_slot == wanted), 1.0, 0.0).astype(jnp.bfloat16)
        outside = jnp.where(same & (beside == wanted), 1.0, 0.0).astype(jnp.bfloat16)
        lanes = slice(shift * COLS, (shift + 1) * COLS)
        matrix_ref[0:COLS, lanes] = inside
        matrix_ref[COLS : 2 * COLS, lanes] = inside
        matrix_ref[2 * COLS : DEPTH, lanes] = outside
    for part in range(2):
        for group in range(GROUPS):
            start = (GROUPS * part + group) * COLS
            turned_off[start : start + COLS] = off_ref[part, 8 * group : 8 * group + 8].reshape(COLS, COLS).T


def cubic_weights(frac):
    return (
        -frac * (frac - 1.0) * (frac - 2.0) * (1.0 / 6.0),
        (frac + 1.0) * (frac - 1.0) * (frac - 2.0) * 0.5,
        (frac + 1.0) * frac * (frac - 2.0) * -0.5,
        (frac + 1.0) * frac * (frac - 1.0) * (1.0 / 6.0),
    )


def rotated(weights, odd, half):
    once = [jnp.where(odd, weights[(k - 1) % 4], weights[k]) for k in range(4)]
    return [jnp.where(half, once[(k - 2) % 4], once[k]) for k in range(4)]


def middle_pair(values, odd, half):
    one = jnp.where(half, values[3], values[1])
    two = jnp.where(half, values[0], values[2])
    three = jnp.where(half, values[1], values[3])
    return jnp.where(odd, two, one), jnp.where(odd, three, two)


def weighted(taps, col_weights, row_weights):
    sums = [None] * 4
    for q in range(4):
        for p in range(4):
            term = col_weights[q] * taps[q][p]
            sums[p] = term if sums[p] is None else sums[p] + term
    total = row_weights[0] * sums[0]
    for p in range(1, 4):
        total = total + row_weights[p] * sums[p]
    return total


def advect_block(load, col_off, row_off, wind_here, emit):
    row_start = 2 - row_off
    col_start = 6 - col_off
    row_low = [row_start <= p for p in range(4)]
    col_low = [col_start <= q for q in range(4)]
    col_mid = [col_start <= q + 4 for q in range(4)]
    row_odd = (row_start & 1) != 0
    row_half = (row_start & 2) != 0
    col_odd = (col_start & 1) != 0
    col_half = (col_start & 2) != 0
    col_float = col_off.astype(jnp.float32)
    row_float = row_off.astype(jnp.float32)

    def column_class(field, q):
        picked = []
        for p in range(4):
            parts = [
                jnp.where(row_low[p], load(field, p, k), load(field, p + 4, k))
                for k in (q, q + 4, q + 8)
            ]
            picked.append(
                jnp.where(col_low[q], parts[0], jnp.where(col_mid[q], parts[1], parts[2]))
            )
        return picked

    wind_taps = [[column_class(field, q) for q in range(4)] for field in range(WINDS)]
    cells = []
    for field in range(WINDS):
        lows = []
        highs = []
        for q in range(4):
            low, high = middle_pair(wind_taps[field][q], row_odd, row_half)
            lows.append(low)
            highs.append(high)
        low_left, low_right = middle_pair(lows, col_odd, col_half)
        up_left, up_right = middle_pair(highs, col_odd, col_half)
        cells.append((low_left, low_right - low_left, up_left, up_right - up_left))
    disp = wind_here
    for repeat in range(2):
        frac_x = jnp.clip(col_float - disp[0], 0.0, 1.0)
        frac_y = jnp.clip(row_float - disp[1], 0.0, 1.0)
        moved = []
        for field in range(WINDS):
            low_left, low_step, up_left, up_step = cells[field]
            low = low_left + frac_x * low_step
            up = up_left + frac_x * up_step
            depart = low + frac_y * (up - low)
            moved.append(0.5 * (wind_here[field] + depart))
        disp = moved
    frac_x = jnp.clip(col_float - disp[0], 0.0, 1.0)
    frac_y = jnp.clip(row_float - disp[1], 0.0, 1.0)
    col_weights = rotated(cubic_weights(frac_x), col_odd, col_half)
    row_weights = rotated(cubic_weights(frac_y), row_odd, row_half)
    for field in range(FIELDS):
        if field < WINDS:
            taps = wind_taps[field]
        else:
            taps = [column_class(field, q) for q in range(4)]
        emit(field, weighted(taps, col_weights, row_weights))


def block_access(shifted, base, height):
    def load(field, row, k):
        return shifted[pl.ds(base + ((GROUPS * 8 * field + row) * height + 1 + k), 8)]

    here = [load(field, 3, 7) for field in range(WINDS)]
    return load, here


def interior(own_ref, off_ref, matrix_ref, t1_ref, t2_ref, result, beside, around, shifted):
    lat_even = parities()[1]
    low_half = lax.broadcasted_iota(jnp.int32, (8, COLS), 0) < 4
    for edge in range(EDGE):
        field, group = divmod(edge, GROUPS)
        pieces = []
        for lev in range(8):
            line = 4 * (field * LEVS + 8 * group + lev)
            one = [t_ref[line + 8 : line + 16] for t_ref in (t1_ref, t2_ref)]
            two = [t_ref[line + 4 : line + 12] for t_ref in (t1_ref, t2_ref)]
            south_one = pick(lat_even, one[0], one[1])
            south_two = pick(lat_even, two[0], two[1])
            north_one = pick(lat_even, one[1], one[0])
            north_two = pick(lat_even, two[1], two[0])
            pieces.append(jnp.where(low_half, whole(south_one), south_two - whole(south_two)))
            pieces.append(jnp.where(low_half, north_one - whole(north_one), whole(north_two)))
        turned = jnp.concatenate(pieces, axis=0).T.astype(jnp.bfloat16)
        around[edge] = turned
        beside[edge, 0:16] = turned[0:16]
        beside[edge, 16:32] = turned[COLS - 16 : COLS]
    for pair in range(4):
        lanes = slice(2 * COLS * pair, 2 * COLS * (pair + 1))
        rows = jnp.concatenate([own_ref[...], around[...]], axis=2).reshape(EDGE * COLS, DEPTH)
        spread = jnp.dot(rows, matrix_ref[:, lanes], preferred_element_type=jnp.float32)
        for edge in range(EDGE):
            for half in range(2):
                start = (8 * edge + 2 * pair + half) * TALL
                shifted[start : start + COLS] = spread[
                    edge * COLS : (edge + 1) * COLS, half * COLS : (half + 1) * COLS
                ]

    def step(index, carry):
        group = index // 14
        start = 8 * (index % 14)
        load, here = block_access(shifted, group * (8 * TALL) + start, TALL)
        place = pl.multiple_of(group * COLS + start + 8, 8)

        def emit(field, value):
            result[pl.ds(pl.multiple_of(place + GROUPS * COLS * field, 8), 8)] = value

        advect_block(load, off_ref[pl.ds(place, 8)], off_ref[pl.ds(pl.multiple_of(place + GROUPS * COLS, 8), 8)], here, emit)
        return carry

    lax.fori_loop(0, GROUPS * 14, step, 0, unroll=3)


def early_kernel(own_ref, off_ref, matrix_ref, t1_ref, t2_ref, back_in, result, beside, back_out, around, shifted):
    @pl.when(lax.axis_index("lon") % EARLY == 0)
    def _():
        interior(own_ref, off_ref, matrix_ref, t1_ref, t2_ref, result, beside, around, shifted)


def late_kernel(
    own_ref, off_ref, matrix_ref, t1_ref, t2_ref, forth, result_in, beside_in, result, beside, around, shifted
):
    early = lax.axis_index("lon") % EARLY == 0

    @pl.when(early)
    def _():
        result[...] = result_in[...]
        beside[...] = beside_in[...]

    @pl.when(jnp.logical_not(early))
    def _():
        interior(own_ref, off_ref, matrix_ref, t1_ref, t2_ref, result, beside, around, shifted)


def edge_work(
    own_ref, off_ref, matrix_ref, beside, result, a_ref, forth_ref, back_ref, out_ref, rows, shifted, staged, sems
):
    lon_even = parities()[0]
    slot = lane_slot((8, COLS))

    def sides(place):
        west = forth_ref[place] if back_ref is None else pick(lon_even, forth_ref[place], a_ref[place])
        east = a_ref[place] if back_ref is None else pick(lon_even, a_ref[place], back_ref[place])
        return west, east

    for packed in range(SIDE):
        north = sides(EDGE + packed)
        south = sides(EDGE + SIDE + packed)
        for part in range(min(4, EDGE - 4 * packed)):
            edge = 4 * packed + part
            outer = []
            for side in range(2):
                above = pltpu.roll(north[side], 12 - 4 * part, 1) if part != 3 else north[side]
                below = pltpu.roll(south[side], -4 * part % COLS, 1) if part else south[side]
                both = jnp.where(slot >= 12, above, below)
                rest = both - whole(both)
                rest = jnp.where(slot < 8, pltpu.roll(rest, 4, 1), pltpu.roll(rest, COLS - 4, 1))
                outer.append(jnp.where((slot >= 4) & (slot < 12), rest, both))
            rows[edge, 0:16, 0 : 2 * COLS] = own_ref[edge, 0:16]
            rows[edge, 16:32, 0 : 2 * COLS] = own_ref[edge, COLS - 16 : COLS]
            rows[edge, 0:32, 2 * COLS : DEPTH] = beside[edge]
            rows[edge, 32:48, 0 : 2 * COLS] = jnp.concatenate(
                split(jnp.concatenate(sides(edge), axis=0)), axis=1
            )
            rows[edge, 32:48, 2 * COLS : DEPTH] = jnp.concatenate(outer, axis=0).astype(jnp.bfloat16)
    for pair in range(4):
        lanes = slice(2 * COLS * pair, 2 * COLS * (pair + 1))
        spread = jnp.dot(
            rows[...].reshape(EDGE * 2 * STRIP, DEPTH), matrix_ref[:, lanes], preferred_element_type=jnp.float32
        )
        for edge in range(EDGE):
            for half in range(2):
                part = spread[edge * 2 * STRIP : (edge + 1) * 2 * STRIP, half * COLS : (half + 1) * COLS]
                start = (8 * edge + 2 * pair + half) * 2 * STRIP
                shifted[start : start + 8] = part[32:40]
                shifted[start + 8 : start + 40] = part[0:32]
                shifted[start + 40 : start + 48] = part[40:48]

    copies = []
    for group in range(GROUPS):
        values = {}
        for side in range(2):
            target = (COLS - 8) * side + COLS * group
            other = target + GROUPS * COLS
            load, here = block_access(shifted, (16 * group + side) * STRIP, 2 * STRIP)

            def emit(field, value):
                values[field, side] = value

            advect_block(load, off_ref[target : target + 8], off_ref[other : other + 8], here, emit)
        for field in range(FIELDS):
            start = (GROUPS * field + group) * COLS
            whole_block = jnp.concatenate(
                [values[field, 0], result[start + 8 : start + COLS - 8], values[field, 1]], axis=0
            )
            staged[group, field] = whole_block.T.reshape(8, ROWS, COLS)
            copies.append(
                pltpu.make_async_copy(
                    staged.at[group, field], out_ref.at[field, pl.ds(8 * group, 8)], sems.at[group, field]
                )
            )
            copies[-1].start()
    for copy in copies:
        copy.wait()


def early_edge_kernel(own_ref, off_ref, matrix_ref, beside, result, a_ref, forth_ref, out_ref, *scratch):
    @pl.when(lax.axis_index("lon") % EARLY == 0)
    def _():
        edge_work(own_ref, off_ref, matrix_ref, beside, result, a_ref, forth_ref, None, out_ref, *scratch)


def late_edge_kernel(
    own_ref, off_ref, matrix_ref, beside, result, a_ref, forth_ref, back_ref, out_in, out_ref, *scratch
):
    @pl.when(lax.axis_index("lon") % EARLY != 0)
    def _():
        edge_work(own_ref, off_ref, matrix_ref, beside, result, a_ref, forth_ref, back_ref, out_ref, *scratch)


def cost(flops):
    return pl.CostEstimate(flops=flops, bytes_accessed=10**6, transcendentals=0)


def shards(wind, tracers, cell_off):
    f32 = jnp.float32
    vmem = pl.BlockSpec(memory_space=pltpu.VMEM)
    anywhere = pl.BlockSpec(memory_space=pl.ANY)
    params = pltpu.CompilerParams(vmem_limit_bytes=VMEM_LIMIT)
    sds = jax.ShapeDtypeStruct
    hbm = pl.BlockSpec(memory_space=pltpu.HBM)
    hbm = pl.BlockSpec(memory_space=pltpu.HBM)
    direct = pltpu.CompilerParams(vmem_limit_bytes=PACK_LIMIT)
    lat_shape = sds((MAIN + NARROW, COLS), f32)
    cells_shape = pltpu.VMEM((FIELDS, LEVS, ROWS, COLS), f32)
    edges, t1, t2 = pl.pallas_call(
        pack_kernel,
        out_shape=(sds((2 * EDGE, 8, COLS), f32), lat_shape, lat_shape),
        in_specs=[hbm] * 2,
        out_specs=(vmem,) * 3,
        scratch_shapes=[cells_shape, pltpu.SemaphoreType.DMA((FIELDS,))],
        compiler_params=direct,
        name="pack",
    )(wind, tracers)
    count = lax.axis_size("lon")
    lon_pairs = [(i, i ^ 1) for i in range(count)]
    lon_forth = [(i, (i + 1) % count) for i in range(1, count, 2)]
    lon_back = [(i, (i - 1) % count) for i in range(0, count, 2)]
    lats = lax.axis_size("lat")
    lat_pairs = [(i, i ^ 1) for i in range(lats)]
    lat_middle = [(i, i + 1 if i % 2 else i - 1) for i in range(1, lats - 1)]
    t1 = lax.ppermute(t1, "lat", lat_pairs)
    t2 = lax.ppermute(t2, "lat", lat_middle)
    own, turned_off, matrix = pl.pallas_call(
        own_kernel,
        out_shape=(
            sds((EDGE, COLS, 2 * COLS), jnp.bfloat16),
            sds((2 * GROUPS * COLS, COLS), jnp.int32),
            sds((DEPTH, 8 * COLS), jnp.bfloat16),
        ),
        in_specs=[vmem] * 3,
        out_specs=(vmem,) * 3,
        compiler_params=params,
        cost_estimate=cost(2 * 10**10),
        name="own",
    )(wind, tracers, cell_off)
    side_shape = sds((PAYLOAD, 8, COLS), f32)
    side_a, forth, back = pl.pallas_call(
        side_kernel,
        out_shape=(side_shape,) * 3,
        in_specs=[vmem] * 3,
        out_specs=(vmem,) * 3,
        compiler_params=params,
        name="sides",
    )(edges, t1, t2)
    side_a = lax.ppermute(side_a, "lon", lon_pairs)
    forth = lax.ppermute(forth, "lon", lon_forth)
    result_shapes = (sds((EDGE * COLS, COLS), f32), sds((EDGE, 32, COLS), jnp.bfloat16))
    scratch = [pltpu.VMEM((EDGE, COLS, COLS), jnp.bfloat16), pltpu.VMEM((EDGE * 8 * TALL, COLS), f32)]
    result, beside, back = pl.pallas_call(
        early_kernel,
        out_shape=result_shapes + (side_shape,),
        in_specs=[vmem] * 5 + [anywhere],
        out_specs=(vmem, vmem, anywhere),
        scratch_shapes=scratch,
        input_output_aliases={5: 2},
        compiler_params=params,
        cost_estimate=cost(10**10),
        name="early",
    )(own, turned_off, matrix, t1, t2, back)
    back = lax.ppermute(back, "lon", lon_back)
    edge_scratch = [
        pltpu.VMEM((EDGE, 2 * STRIP, DEPTH), jnp.bfloat16),
        pltpu.VMEM((EDGE * 8 * 2 * STRIP, COLS), f32),
        pltpu.VMEM((GROUPS, FIELDS, 8, ROWS, COLS), f32),
        pltpu.SemaphoreType.DMA((GROUPS, FIELDS)),
    ]
    out = pl.pallas_call(
        early_edge_kernel,
        out_shape=sds((FIELDS, LEVS, ROWS, COLS), f32),
        in_specs=[vmem] * 7,
        out_specs=anywhere,
        scratch_shapes=edge_scratch,
        compiler_params=params,
        cost_estimate=cost(10**10),
        name="early_edges",
    )(own, turned_off, matrix, beside, result, side_a, forth)
    result, beside = pl.pallas_call(
        late_kernel,
        out_shape=result_shapes,
        in_specs=[vmem] * 5 + [anywhere] + [vmem] * 2,
        out_specs=(vmem, vmem),
        scratch_shapes=scratch,
        compiler_params=params,
        cost_estimate=cost(10**10),
        name="late",
    )(own, turned_off, matrix, t1, t2, forth, result, beside)
    return pl.pallas_call(
        late_edge_kernel,
        out_shape=sds((FIELDS, LEVS, ROWS, COLS), f32),
        in_specs=[vmem] * 8 + [anywhere],
        out_specs=anywhere,
        scratch_shapes=edge_scratch,
        input_output_aliases={8: 0},
        compiler_params=params,
        name="late_edges",
    )(own, turned_off, matrix, beside, result, side_a, forth, back, out)


def solution(mesh):
    placed = P(None, None, "lat", "lon")
    return jax.shard_map(shards, mesh=mesh, in_specs=(placed,) * 3, out_specs=placed, check_vma=False)
```

```python
import jax
import jax.numpy as jnp
from jax import lax
from jax.experimental import pallas as pl
from jax.experimental.pallas import tpu as pltpu
from jax.sharding import PartitionSpec as P

LEVS = 24
ROWS = 16
COLS = 128
WINDS = 2
FIELDS = 6
GROUPS = 3
EDGE = FIELDS * GROUPS
WIDE = COLS + 16
DEPTH = 3 * COLS
SIDE = -(-EDGE // 4)
MAIN = 8 * (FIELDS * LEVS // 2 + 2)
NARROW = 2 * 8 * SIDE
PAYLOAD = EDGE + 2 * SIDE
STRIP = 24
STRIDE = 2 * STRIP + 8
TALL = COLS + 8
EARLY = 16
VMEM_LIMIT = 24 * 1024 * 1024
PACK_LIMIT = 60 * 1024 * 1024


def parities():
    return lax.axis_index("lon") % 2 == 0, lax.axis_index("lat") % 2 == 0


def pick(flag, first, second):
    return jnp.where(jnp.full(first.shape, flag), first, second)


def lane_slot(shape):
    return lax.broadcasted_iota(jnp.int32, shape, len(shape) - 1) % 16


def split(values):
    high = values.astype(jnp.bfloat16)
    return high, (values - high.astype(jnp.float32)).astype(jnp.bfloat16)


def whole(values):
    return values.astype(jnp.bfloat16).astype(jnp.float32)


def load_fields(wind_hbm, tracer_hbm, cells, sems):
    copies = []
    for field in range(FIELDS):
        source = wind_hbm.at[field] if field < WINDS else tracer_hbm.at[field - WINDS]
        copies.append(pltpu.make_async_copy(source, cells.at[field], sems.at[field]))
    for copy in copies:
        copy.start()
    return copies


def pack_kernel(wind_hbm, tracer_hbm, edges, t1_ref, t2_ref, cells, sems):
    lat_even = parities()[1]
    low_half = lax.broadcasted_iota(jnp.int32, (8, COLS), 0) < 4
    slot = lane_slot((8, COLS))
    zero = jnp.zeros((8, COLS), jnp.float32)
    copies = load_fields(wind_hbm, tracer_hbm, cells, sems)

    def put(start, top, bottom):
        t1_ref[start : start + 8] = pick(lat_even, bottom, top)
        t2_ref[start : start + 8] = pick(lat_even, top, bottom)

    put(0, zero, zero)
    t2_ref[MAIN + NARROW : MAIN + NARROW + 8] = zero
    put(MAIN - 8, zero, zero)
    for field in range(FIELDS):
        copies[field].wait()
        for group in range(GROUPS):
            turned = cells[field, 8 * group : 8 * group + 8].reshape(COLS, COLS).T
            edges[GROUPS * field + group] = turned[0:8]
            edges[EDGE + GROUPS * field + group] = turned[COLS - 8 : COLS]
        for pair in range(LEVS // 2):
            first = cells[field, 2 * pair]
            second = cells[field, 2 * pair + 1]
            top = jnp.where(low_half, first[0:8], pltpu.roll(second[0:8], 4, 0))
            bottom = jnp.where(low_half, pltpu.roll(first[8:16], 4, 0), second[8:16])
            put(8 * (field * LEVS // 2 + pair + 1), top, bottom)
    for side in range(2):
        for packed in range(SIDE):
            top = None
            bottom = None
            for part in range(min(4, EDGE - 4 * packed)):
                piece = edges[EDGE * side + 4 * packed + part]
                upper = pltpu.roll(piece, 4 * part, 1) if part else piece
                lower = pltpu.roll(piece, (4 * part - 12) % COLS, 1) if part != 3 else piece
                here = (slot >= 4 * part) & (slot < 4 * part + 4)
                top = upper if top is None else jnp.where(here, upper, top)
                bottom = lower if bottom is None else jnp.where(here, lower, bottom)
            put(MAIN + 8 * (SIDE * side + packed), top, bottom)


def side_kernel(edges, t1_ref, t2_ref, a_ref, forth_ref, back_ref):
    lon_even, lat_even = parities()

    def put(place, west, east):
        a_ref[place] = pick(lon_even, east, west)
        other = pick(lon_even, west, east)
        forth_ref[place] = other
        back_ref[place] = other

    for edge in range(EDGE):
        put(edge, edges[edge], edges[EDGE + edge])
    for packed in range(SIDE):
        north = []
        south = []
        for side in range(2):
            start = MAIN + 8 * (SIDE * side + packed)
            first = t1_ref[start : start + 8]
            second = t2_ref[start : start + 8]
            north.append(pick(lat_even, second, first))
            south.append(pick(lat_even, first, second))
        put(EDGE + packed, *north)
        put(EDGE + SIDE + packed, *south)


def own_kernel(wind_ref, tracer_ref, off_ref, own_ref, turned_off, matrix_ref):
    for field in range(FIELDS):
        ref, inner = (wind_ref, field) if field < WINDS else (tracer_ref, field - WINDS)
        for group in range(GROUPS):
            turned = ref[inner, 8 * group : 8 * group + 8].reshape(COLS, COLS).T
            own_ref[GROUPS * field + group] = jnp.concatenate(split(turned), axis=1)
    source = lax.broadcasted_iota(jnp.int32, (COLS, COLS), 0)
    target = lax.broadcasted_iota(jnp.int32, (COLS, COLS), 1)
    source_slot = source % 16
    beside = jnp.where(source_slot < 8, 16 + source_slot % 4, source_slot % 4 - 4)
    same = source // 16 == target // 16
    for shift in range(8):
        wanted = target % 16 + (shift - 3)
        inside = jnp.where(same & (source_slot == wanted), 1.0, 0.0).astype(jnp.bfloat16)
        outside = jnp.where(same & (beside == wanted), 1.0, 0.0).astype(jnp.bfloat16)
        lanes = slice(shift * COLS, (shift + 1) * COLS)
        matrix_ref[0:COLS, lanes] = inside
        matrix_ref[COLS : 2 * COLS, lanes] = inside
        matrix_ref[2 * COLS : DEPTH, lanes] = outside
    for part in range(2):
        for group in range(GROUPS):
            start = (GROUPS * part + group) * COLS
            turned_off[start : start + COLS] = off_ref[part, 8 * group : 8 * group + 8].reshape(COLS, COLS).T


def cubic_weights(frac):
    return (
        -frac * (frac - 1.0) * (frac - 2.0) * (1.0 / 6.0),
        (frac + 1.0) * (frac - 1.0) * (frac - 2.0) * 0.5,
        (frac + 1.0) * frac * (frac - 2.0) * -0.5,
        (frac + 1.0) * frac * (frac - 1.0) * (1.0 / 6.0),
    )


def rotated(weights, odd, half):
    once = [jnp.where(odd, weights[(k - 1) % 4], weights[k]) for k in range(4)]
    return [jnp.where(half, once[(k - 2) % 4], once[k]) for k in range(4)]


def middle_pair(values, odd, half):
    one = jnp.where(half, values[3], values[1])
    two = jnp.where(half, values[0], values[2])
    three = jnp.where(half, values[1], values[3])
    return jnp.where(odd, two, one), jnp.where(odd, three, two)


def weighted(taps, col_weights, row_weights):
    sums = [None] * 4
    for q in range(4):
        for p in range(4):
            term = col_weights[q] * taps[q][p]
            sums[p] = term if sums[p] is None else sums[p] + term
    total = row_weights[0] * sums[0]
    for p in range(1, 4):
        total = total + row_weights[p] * sums[p]
    return total


def advect_block(load, col_off, row_off, wind_here, emit):
    row_start = 2 - row_off
    col_start = 6 - col_off
    row_low = [row_start <= p for p in range(4)]
    col_low = [col_start <= q for q in range(4)]
    col_mid = [col_start <= q + 4 for q in range(4)]
    row_odd = (row_start & 1) != 0
    row_half = (row_start & 2) != 0
    col_odd = (col_start & 1) != 0
    col_half = (col_start & 2) != 0
    col_float = col_off.astype(jnp.float32)
    row_float = row_off.astype(jnp.float32)

    def column_class(field, q):
        picked = []
        for p in range(4):
            parts = [
                jnp.where(row_low[p], load(field, p, k), load(field, p + 4, k))
                for k in (q, q + 4, q + 8)
            ]
            picked.append(
                jnp.where(col_low[q], parts[0], jnp.where(col_mid[q], parts[1], parts[2]))
            )
        return picked

    wind_taps = [[column_class(field, q) for q in range(4)] for field in range(WINDS)]
    cells = []
    for field in range(WINDS):
        lows = []
        highs = []
        for q in range(4):
            low, high = middle_pair(wind_taps[field][q], row_odd, row_half)
            lows.append(low)
            highs.append(high)
        low_left, low_right = middle_pair(lows, col_odd, col_half)
        up_left, up_right = middle_pair(highs, col_odd, col_half)
        cells.append((low_left, low_right - low_left, up_left, up_right - up_left))
    disp = wind_here
    for repeat in range(2):
        frac_x = jnp.clip(col_float - disp[0], 0.0, 1.0)
        frac_y = jnp.clip(row_float - disp[1], 0.0, 1.0)
        moved = []
        for field in range(WINDS):
            low_left, low_step, up_left, up_step = cells[field]
            low = low_left + frac_x * low_step
            up = up_left + frac_x * up_step
            depart = low + frac_y * (up - low)
            moved.append(0.5 * (wind_here[field] + depart))
        disp = moved
    frac_x = jnp.clip(col_float - disp[0], 0.0, 1.0)
    frac_y = jnp.clip(row_float - disp[1], 0.0, 1.0)
    col_weights = rotated(cubic_weights(frac_x), col_odd, col_half)
    row_weights = rotated(cubic_weights(frac_y), row_odd, row_half)
    for field in range(FIELDS):
        if field < WINDS:
            taps = wind_taps[field]
        else:
            taps = [column_class(field, q) for q in range(4)]
        emit(field, weighted(taps, col_weights, row_weights))


def block_access(shifted, base, height):
    def load(field, row, k):
        return shifted[pl.ds(base + ((GROUPS * 8 * field + row) * height + 1 + k), 8)]

    here = [load(field, 3, 7) for field in range(WINDS)]
    return load, here


def interior(own_ref, off_ref, matrix_ref, t1_ref, t2_ref, result, beside, around, shifted):
    lat_even = parities()[1]
    low_half = lax.broadcasted_iota(jnp.int32, (8, COLS), 0) < 4
    for edge in range(EDGE):
        field, group = divmod(edge, GROUPS)
        pieces = []
        for lev in range(8):
            line = 4 * (field * LEVS + 8 * group + lev)
            one = [t_ref[line + 8 : line + 16] for t_ref in (t1_ref, t2_ref)]
            two = [t_ref[line + 4 : line + 12] for t_ref in (t1_ref, t2_ref)]
            south_one = pick(lat_even, one[0], one[1])
            south_two = pick(lat_even, two[0], two[1])
            north_one = pick(lat_even, one[1], one[0])
            north_two = pick(lat_even, two[1], two[0])
            pieces.append(jnp.where(low_half, whole(south_one), south_two - whole(south_two)))
            pieces.append(jnp.where(low_half, north_one - whole(north_one), whole(north_two)))
        turned = jnp.concatenate(pieces, axis=0).T.astype(jnp.bfloat16)
        around[edge] = turned
        beside[edge, 0:16] = turned[0:16]
        beside[edge, 16:32] = turned[COLS - 16 : COLS]
    for pair in range(4):
        lanes = slice(2 * COLS * pair, 2 * COLS * (pair + 1))
        rows = jnp.concatenate([own_ref[...], around[...]], axis=2).reshape(EDGE * COLS, DEPTH)
        spread = jnp.dot(rows, matrix_ref[:, lanes], preferred_element_type=jnp.float32)
        for edge in range(EDGE):
            for half in range(2):
                start = (8 * edge + 2 * pair + half) * TALL
                shifted[start : start + COLS] = spread[
                    edge * COLS : (edge + 1) * COLS, half * COLS : (half + 1) * COLS
                ]

    def step(index, carry):
        group = index // 14
        start = 8 * (index % 14)
        load, here = block_access(shifted, group * (8 * TALL) + start, TALL)
        place = pl.multiple_of(group * COLS + start + 8, 8)

        def emit(field, value):
            result[pl.ds(pl.multiple_of(place + GROUPS * COLS * field, 8), 8)] = value

        advect_block(load, off_ref[pl.ds(place, 8)], off_ref[pl.ds(pl.multiple_of(place + GROUPS * COLS, 8), 8)], here, emit)
        return carry

    lax.fori_loop(0, GROUPS * 14, step, 0, unroll=3)


def early_kernel(own_ref, off_ref, matrix_ref, t1_ref, t2_ref, back_in, result, beside, back_out, around, shifted):
    @pl.when(lax.axis_index("lon") % EARLY == 0)
    def _():
        interior(own_ref, off_ref, matrix_ref, t1_ref, t2_ref, result, beside, around, shifted)


def late_kernel(
    own_ref, off_ref, matrix_ref, t1_ref, t2_ref, forth, result_in, beside_in, result, beside, around, shifted
):
    early = lax.axis_index("lon") % EARLY == 0

    @pl.when(early)
    def _():
        result[...] = result_in[...]
        beside[...] = beside_in[...]

    @pl.when(jnp.logical_not(early))
    def _():
        interior(own_ref, off_ref, matrix_ref, t1_ref, t2_ref, result, beside, around, shifted)


def edge_work(
    own_ref, off_ref, matrix_ref, beside, result, a_ref, b_refs, out_ref, rows, shifted, staged, sems
):
    lon_even = parities()[0]
    slot = lane_slot((8, COLS))

    late = lax.axis_index("lon") % EARLY == EARLY - 1

    def sides(place):
        if len(b_refs) == 1:
            return b_refs[0][place], a_ref[place]
        swapped = b_refs[0][place]
        west = pick(lon_even, swapped, a_ref[place])
        east = pick(lon_even, a_ref[place], pick(late, b_refs[1][place], swapped))
        return west, east

    for packed in range(SIDE):
        north = sides(EDGE + packed)
        south = sides(EDGE + SIDE + packed)
        for part in range(min(4, EDGE - 4 * packed)):
            edge = 4 * packed + part
            outer = []
            for side in range(2):
                above = pltpu.roll(north[side], 12 - 4 * part, 1) if part != 3 else north[side]
                below = pltpu.roll(south[side], -4 * part % COLS, 1) if part else south[side]
                both = jnp.where(slot >= 12, above, below)
                rest = both - whole(both)
                rest = jnp.where(slot < 8, pltpu.roll(rest, 4, 1), pltpu.roll(rest, COLS - 4, 1))
                outer.append(jnp.where((slot >= 4) & (slot < 12), rest, both))
            rows[edge, 0:16, 0 : 2 * COLS] = own_ref[edge, 0:16]
            rows[edge, 16:32, 0 : 2 * COLS] = own_ref[edge, COLS - 16 : COLS]
            rows[edge, 0:32, 2 * COLS : DEPTH] = beside[edge]
            rows[edge, 32:48, 0 : 2 * COLS] = jnp.concatenate(
                split(jnp.concatenate(sides(edge), axis=0)), axis=1
            )
            rows[edge, 32:48, 2 * COLS : DEPTH] = jnp.concatenate(outer, axis=0).astype(jnp.bfloat16)
    for pair in range(4):
        lanes = slice(2 * COLS * pair, 2 * COLS * (pair + 1))
        spread = jnp.dot(
            rows[...].reshape(EDGE * 2 * STRIP, DEPTH), matrix_ref[:, lanes], preferred_element_type=jnp.float32
        )
        for edge in range(EDGE):
            for half in range(2):
                part = spread[edge * 2 * STRIP : (edge + 1) * 2 * STRIP, half * COLS : (half + 1) * COLS]
                start = (8 * edge + 2 * pair + half) * STRIDE
                shifted[start : start + 8] = part[32:40]
                shifted[start + 8 : start + 40] = part[0:32]
                shifted[start + 40 : start + 48] = part[40:48]

    copies = []
    for group in range(GROUPS):
        values = {}
        for side in range(2):
            target = (COLS - 8) * side + COLS * group
            other = target + GROUPS * COLS
            load, here = block_access(shifted, 8 * STRIDE * group + STRIP * side, STRIDE)

            def emit(field, value):
                values[field, side] = value

            advect_block(load, off_ref[target : target + 8], off_ref[other : other + 8], here, emit)
        for field in range(FIELDS):
            start = (GROUPS * field + group) * COLS
            whole_block = jnp.concatenate(
                [values[field, 0], result[start + 8 : start + COLS - 8], values[field, 1]], axis=0
            )
            staged[group, field] = whole_block.T.reshape(8, ROWS, COLS)
            copies.append(
                pltpu.make_async_copy(
                    staged.at[group, field], out_ref.at[field, pl.ds(8 * group, 8)], sems.at[group, field]
                )
            )
            copies[-1].start()
    for copy in copies:
        copy.wait()


def early_edge_kernel(own_ref, off_ref, matrix_ref, beside, result, a_ref, forth_ref, out_ref, *scratch):
    @pl.when(lax.axis_index("lon") % EARLY == 0)
    def _():
        edge_work(own_ref, off_ref, matrix_ref, beside, result, a_ref, (forth_ref,), out_ref, *scratch)


def late_edge_kernel(
    own_ref, off_ref, matrix_ref, beside, result, a_ref, swap_ref, back_ref, out_in, out_ref, *scratch
):
    @pl.when(lax.axis_index("lon") % EARLY != 0)
    def _():
        edge_work(own_ref, off_ref, matrix_ref, beside, result, a_ref, (swap_ref, back_ref), out_ref, *scratch)


def cost(flops):
    return pl.CostEstimate(flops=flops, bytes_accessed=10**6, transcendentals=0)


def shards(wind, tracers, cell_off):
    f32 = jnp.float32
    vmem = pl.BlockSpec(memory_space=pltpu.VMEM)
    anywhere = pl.BlockSpec(memory_space=pl.ANY)
    params = pltpu.CompilerParams(vmem_limit_bytes=VMEM_LIMIT)
    sds = jax.ShapeDtypeStruct
    hbm = pl.BlockSpec(memory_space=pltpu.HBM)
    hbm = pl.BlockSpec(memory_space=pltpu.HBM)
    direct = pltpu.CompilerParams(vmem_limit_bytes=PACK_LIMIT)
    lat_shape = sds((MAIN + NARROW, COLS), f32)
    cells_shape = pltpu.VMEM((FIELDS, LEVS, ROWS, COLS), f32)
    edges, t1, t2 = pl.pallas_call(
        pack_kernel,
        out_shape=(sds((2 * EDGE, 8, COLS), f32), lat_shape, sds((MAIN + NARROW + 8, COLS), f32)),
        in_specs=[hbm] * 2,
        out_specs=(vmem,) * 3,
        scratch_shapes=[cells_shape, pltpu.SemaphoreType.DMA((FIELDS,))],
        compiler_params=direct,
        name="pack",
    )(wind, tracers)
    count = lax.axis_size("lon")
    lon_pairs = [(i, i ^ 1) for i in range(count)]
    lon_forth = [(i, (i + 1) % count) for i in range(EARLY - 1, count, EARLY)]
    lon_back = [(i, (i - 1) % count) for i in range(0, count, EARLY)]
    lon_swap = [(i, i + 1 if i % 2 else i - 1) for i in range(count) if 0 < i % EARLY < EARLY - 1]
    lats = lax.axis_size("lat")
    lat_pairs = [(i, i ^ 1) for i in range(lats)]
    lat_middle = [(i, i + 1 if i % 2 else i - 1) for i in range(1, lats - 1)]
    t1 = lax.ppermute(t1, "lat", lat_pairs)
    t2 = lax.ppermute(t2, "lat", lat_middle)
    own, turned_off, matrix = pl.pallas_call(
        own_kernel,
        out_shape=(
            sds((EDGE, COLS, 2 * COLS), jnp.bfloat16),
            sds((2 * GROUPS * COLS, COLS), jnp.int32),
            sds((DEPTH, 8 * COLS), jnp.bfloat16),
        ),
        in_specs=[vmem] * 3,
        out_specs=(vmem,) * 3,
        compiler_params=params,
        cost_estimate=cost(2 * 10**10),
        name="own",
    )(wind, tracers, cell_off)
    side_shape = sds((PAYLOAD, 8, COLS), f32)
    side_a, forth, back = pl.pallas_call(
        side_kernel,
        out_shape=(side_shape,) * 3,
        in_specs=[vmem] * 3,
        out_specs=(vmem,) * 3,
        compiler_params=params,
        name="sides",
    )(edges, t1, t2)
    side_a = lax.ppermute(side_a, "lon", lon_pairs)
    swap = lax.ppermute(forth, "lon", lon_swap)
    forth = lax.ppermute(forth, "lon", lon_forth)
    result_shapes = (sds((EDGE * COLS, COLS), f32), sds((EDGE, 32, COLS), jnp.bfloat16))
    scratch = [pltpu.VMEM((EDGE, COLS, COLS), jnp.bfloat16), pltpu.VMEM((EDGE * 8 * TALL, COLS), f32)]
    result, beside, back = pl.pallas_call(
        early_kernel,
        out_shape=result_shapes + (side_shape,),
        in_specs=[vmem] * 5 + [anywhere],
        out_specs=(vmem, vmem, anywhere),
        scratch_shapes=scratch,
        input_output_aliases={5: 2},
        compiler_params=params,
        cost_estimate=cost(10**10),
        name="early",
    )(own, turned_off, matrix, t1, t2, back)
    back = lax.ppermute(back, "lon", lon_back)
    edge_scratch = [
        pltpu.VMEM((EDGE, 2 * STRIP, DEPTH), jnp.bfloat16),
        pltpu.VMEM((EDGE * 8 * STRIDE, COLS), f32),
        pltpu.VMEM((GROUPS, FIELDS, 8, ROWS, COLS), f32),
        pltpu.SemaphoreType.DMA((GROUPS, FIELDS)),
    ]
    out = pl.pallas_call(
        early_edge_kernel,
        out_shape=sds((FIELDS, LEVS, ROWS, COLS), f32),
        in_specs=[vmem] * 7,
        out_specs=anywhere,
        scratch_shapes=edge_scratch,
        compiler_params=params,
        cost_estimate=cost(10**10),
        name="early_edges",
    )(own, turned_off, matrix, beside, result, side_a, forth)
    result, beside = pl.pallas_call(
        late_kernel,
        out_shape=result_shapes,
        in_specs=[vmem] * 5 + [anywhere] + [vmem] * 2,
        out_specs=(vmem, vmem),
        scratch_shapes=scratch,
        compiler_params=params,
        cost_estimate=cost(10**10),
        name="late",
    )(own, turned_off, matrix, t1, t2, forth, result, beside)
    return pl.pallas_call(
        late_edge_kernel,
        out_shape=sds((FIELDS, LEVS, ROWS, COLS), f32),
        in_specs=[vmem] * 8 + [anywhere],
        out_specs=anywhere,
        scratch_shapes=edge_scratch,
        input_output_aliases={8: 0},
        compiler_params=params,
        name="late_edges",
    )(own, turned_off, matrix, beside, result, side_a, swap, back, out)


def solution(mesh):
    placed = P(None, None, "lat", "lon")
    return jax.shard_map(shards, mesh=mesh, in_specs=(placed,) * 3, out_specs=placed, check_vma=False)
```
